32 devices in a mesh: tmpl: 16 (over z, x, core), tm: 2 (over y).
Axes of the slice: x: 2, y: 2, z: 4, core: 2. Of those that a mesh axis runs over, the one named last changes fastest.
Arguments:
- records: bfloat16 [1536, 1024], P('tmpl', 'tm'), may hold values from -6 to 6
- templates: bfloat16 [2, 512, 48, 200], P(None, 'tmpl'), may hold values from -0.0625 to 0.0625
- channels: int32 [2, 512, 48], P(None, 'tmpl'), may hold values from 0 to 1535
- moveouts: int32 [2, 512, 48], P(None, 'tmpl'), may hold values from 0 to 55
Outputs:
- detections: float32 [2, 512, 1024], P(None, 'tmpl', 'tm')
The draws below stay inside these ranges and needn't reach their ends.
All inputs are finite; a program needn't handle non-finite values.
Results may differ from the reference program's by a relative error of at most 0.0043.
Values may be sent and summed in bfloat16 or wider, within the bound.
A program may use at most 64 MiB of HBM per device.

```python
import math
import jax
import jax.numpy as jnp
from jax import lax

C = 1536
K = 48
L = 200
LAGS = 56
BATCHES = 2
NT_DEV = 32
TIME_DEV = 512
NT = 512
TIME = 1024
N_TMPL = 16
N_TM = 2


def plant(entries, stream_key, least, high):
    dims = entries.shape
    place = [jax.random.randint(jax.random.fold_in(stream_key, axis), (), 0, dims[axis]) for axis in range(len(dims))]
    entries = entries.at[tuple(place)].set(least)
    longest = dims.index(max(dims))
    place[longest] = (place[longest] + 1) % dims[longest]
    return entries.at[tuple(place)].set(high)


def steps_of(own_key, dims, shards, least, largest):
    def one(position, parts):
        draws = jax.random.uniform(jax.random.fold_in(jax.random.fold_in(own_key, 6), position), (parts,), jnp.float32, least / len(shards), largest / len(shards))
        return jnp.repeat(jnp.exp(draws), dims[position] // parts).reshape((-1,) + (1,) * (len(dims) - position - 1))

    factor_of = one(*shards[0])
    for cut in shards[1:]:
        factor_of = factor_of * one(*cut)
    return factor_of


def gaussian(stream_key, extent, spread, limit, pieces=(), kind=jnp.bfloat16):
    values = spread * jax.random.normal(stream_key, extent, jnp.float32)
    if pieces:
        values = values * steps_of(stream_key, extent, pieces, -0.22, 0.18)
    return jnp.clip(values, -limit, limit).astype(kind)


def setup_inputs(seed: int = 0) -> dict:
    splits = jax.random.split(jax.random.key(seed), 5)
    records = gaussian(splits[0], (C, TIME), 1.0, 6.0, ((0, 16), (1, 2)))
    templates = gaussian(splits[1], (BATCHES, NT, K, L), (K * L) ** -0.5, 0.0625, ((1, 16),))
    channels = plant(jax.random.randint(splits[2], (BATCHES, NT, K), 0, C), jax.random.fold_in(splits[2], 1), 0, C - 1).astype(jnp.int32)
    moveouts = plant(jax.random.randint(splits[3], (BATCHES, NT, K), 0, LAGS), jax.random.fold_in(splits[3], 1), 0, LAGS - 1).astype(jnp.int32)
    return {"records": records, "templates": templates, "channels": channels, "moveouts": moveouts}


def tables(count, freqs, width):
    sample = jnp.arange(count, dtype=jnp.int32)[:, None]
    freq = jnp.arange(freqs, dtype=jnp.int32)[None, :]
    angle = (2.0 * math.pi / width) * ((sample * freq) % width).astype(jnp.float32)
    return jnp.concatenate([jnp.cos(angle), jnp.sin(angle)], axis=1)


def reference(records, templates, channels, moveouts):
    width = TIME_DEV + L + LAGS - 2
    freqs = width // 2 + 1
    extra = width - TIME_DEV
    forward = tables(width, freqs, width).astype(jnp.bfloat16)
    inverse = tables(TIME_DEV, freqs, width)
    freq = jnp.arange(freqs, dtype=jnp.int32)
    weight = jnp.where((freq == 0) | (freq == freqs - 1), 1.0, 2.0).astype(jnp.float32) / width
    padded = jnp.pad(records, ((0, 0), (0, extra)))

    def window_spectra(index):
        piece = lax.dynamic_slice_in_dim(padded, (index * TIME_DEV).astype(jnp.int32), width, 1)
        return jnp.dot(piece, forward, preferred_element_type=jnp.float32).astype(jnp.bfloat16)

    spectra = lax.map(window_spectra, jnp.arange(N_TM, dtype=jnp.int32))

    def block(packed):
        waves, chans, lags = packed
        hspec = jnp.dot(waves.reshape(-1, L), forward[:L], preferred_element_type=jnp.float32)
        h_cos, h_sin = hspec[:, :freqs], hspec[:, freqs:]
        angle = (2.0 * math.pi / width) * ((lags.reshape(-1)[:, None] * freq[None, :]) % width).astype(jnp.float32)
        c_theta, s_theta = jnp.cos(angle), jnp.sin(angle)
        rows = chans.reshape(-1)

        def per_window(spec):
            picked = spec[rows].astype(jnp.float32)
            x_cos, x_sin = picked[:, :freqs], picked[:, freqs:]
            prod_a = h_cos * x_cos + h_sin * x_sin
            prod_b = h_sin * x_cos - h_cos * x_sin
            real_part = (prod_a * c_theta - prod_b * s_theta).reshape(NT_DEV, K, freqs).sum(axis=1)
            imag_part = (prod_a * s_theta + prod_b * c_theta).reshape(NT_DEV, K, freqs).sum(axis=1)
            joint = jnp.concatenate([real_part * weight, -imag_part * weight], axis=1)
            return lax.dot_general(joint, inverse, (((1,), (1,)), ((), ())), precision=lax.Precision.HIGHEST)

        outs = lax.map(per_window, spectra)
        return jnp.transpose(outs, (1, 0, 2)).reshape(NT_DEV, N_TM * TIME_DEV)

    blocks = N_TMPL * templates.shape[0]
    waves = templates.reshape(blocks, NT_DEV, K, L)
    chans = channels.reshape(blocks, NT_DEV, K)
    lags = moveouts.reshape(blocks, NT_DEV, K)
    result = lax.map(block, (waves, chans, lags))
    return result.reshape(templates.shape[0], NT_DEV * N_TMPL, N_TM * TIME_DEV)
```

```python
import functools
import math

import jax
import jax.numpy as jnp
import ml_dtypes
import numpy as np
from jax import lax
from jax.experimental import pallas as pl
from jax.experimental.pallas import tpu as pltpu
from jax.sharding import PartitionSpec as P

L = 200
LAGS = 56
SPAN = 256
LANES = 128
SLOTS = 8


def from_behind(block, axis, distance):
    devices = range(lax.axis_size(axis))
    route = [(i - distance, i) for i in devices if i - distance in devices]
    return lax.ppermute(block, axis, route)


def tables(count, freqs, width):
    turn = np.arange(count, dtype=np.int64)[:, None] * np.arange(freqs, dtype=np.int64)[None, :]
    angle = 2.0 * math.pi / width * (turn % width).astype(np.float64)
    return np.concatenate([np.cos(angle), np.sin(angle)], axis=1)


def spread(dst, first, rows, values, slots):
    for piece, slot in enumerate(slots):
        dst[pl.ds(first * SLOTS + slot, rows, stride=SLOTS), :] = values[
            :, piece * LANES : (piece + 1) * LANES
        ]


def waves_spectra(waves_ref, lags_ref, basis_ref, h_ref, rows):
    def step(i, carry):
        first = pl.multiple_of(i * rows, rows)
        wave = waves_ref[pl.ds(first, rows), :].astype(jnp.float32)
        lag = jnp.broadcast_to(lags_ref[pl.ds(first, rows), :], (rows, SPAN))
        bit = 1
        while bit < LAGS:
            wave = jnp.where((lag & bit) != 0, pltpu.roll(wave, bit, 1), wave)
            bit *= 2
        spec = jnp.dot(
            wave.astype(jnp.bfloat16), basis_ref[:SPAN, :], preferred_element_type=jnp.float32
        )
        spread(h_ref, first, rows, spec, (0, 1, 2, 4, 5, 6))
        return carry

    lax.fori_loop(0, waves_ref.shape[0] // rows, step, 0)


def record_spectra(window_ref, basis_ref, x_ref, y_ref, rows):
    def step(i, carry):
        first = pl.multiple_of(i * rows, rows)
        spec = jnp.dot(
            window_ref[pl.ds(first, rows), :], basis_ref[...], preferred_element_type=jnp.float32
        )
        spec = spec.astype(jnp.bfloat16).astype(jnp.float32)
        spread(x_ref, first, rows, spec, (0, 1, 2, 4, 5, 6))
        spread(y_ref, first, rows, spec, (4, 5, 6, 0, 1, 2))
        return carry

    lax.fori_loop(0, window_ref.shape[0] // rows, step, 0)


def correlate(chans_ref, h_ref, x_ref, y_ref, p_ref, q_ref, count, parts):
    def step(t, carry):
        same = [None] * 4
        cross = [None] * 4
        for k in range(parts):
            row = t * parts + k
            chan = pl.multiple_of(chans_ref[row] * SLOTS, SLOTS)
            h = h_ref[pl.ds(pl.multiple_of(row * SLOTS, SLOTS), SLOTS), :]
            a = h * x_ref[pl.ds(chan, SLOTS), :]
            b = h * y_ref[pl.ds(chan, SLOTS), :]
            lane = k % 4
            same[lane] = a if same[lane] is None else same[lane] + a
            cross[lane] = b if cross[lane] is None else cross[lane] + b
        at = pl.ds(pl.multiple_of(t * SLOTS, SLOTS), SLOTS)
        p_ref[at, :] = (same[0] + same[1]) + (same[2] + same[3])
        q_ref[at, :] = (cross[0] + cross[1]) + (cross[2] + cross[3])
        return carry

    lax.fori_loop(0, count, step, 0)


def back(p_ref, q_ref, inverse_ref, out_ref, count):
    real, imag = [], []
    for j in range(3):
        low, high = pl.ds(j, count, stride=SLOTS), pl.ds(j + 4, count, stride=SLOTS)
        real.append(p_ref[low, :] + p_ref[high, :])
        imag.append(q_ref[low, :] - q_ref[high, :])
    joint = jnp.concatenate(real + imag, axis=1)
    out_ref[...] = lax.dot_general(
        joint,
        inverse_ref[...],
        (((1,), (0,)), ((), ())),
        precision=lax.Precision.HIGHEST,
        preferred_element_type=jnp.float32,
    )


def kernel(
    count, parts, chans_ref, window_ref, waves_ref, lags_ref, basis_ref, inverse_ref, out_ref,
    h_ref, x_ref, y_ref, p_ref, q_ref,
):
    waves_spectra(waves_ref, lags_ref, basis_ref, h_ref, 256)
    record_spectra(window_ref, basis_ref, x_ref, y_ref, 256)
    correlate(chans_ref, h_ref, x_ref, y_ref, p_ref, q_ref, count, parts)
    back(p_ref, q_ref, inverse_ref, out_ref, count)


def per_device(records, templates, channels, moveouts):
    time_dev = records.shape[1]
    extra = L + LAGS - 2
    width = time_dev + extra
    freqs = width // 2 + 1
    wide = time_dev + SPAN
    batches, count, parts = channels.shape
    total = batches * count
    rows = total * parts
    forward = np.zeros((wide, 2 * freqs), np.float32)
    forward[:width] = tables(width, freqs, width)
    basis = jnp.asarray(forward.astype(ml_dtypes.bfloat16))
    freq = np.arange(freqs)
    weight = np.where((freq == 0) | (freq == freqs - 1), 1.0, 2.0) / width
    inverse = jnp.asarray(
        (tables(time_dev, freqs, width) * np.concatenate([weight, weight])).T.astype(np.float32)
    )
    rim = from_behind(records[:, :SPAN], "tm", -1)
    window = lax.all_gather(jnp.concatenate([records, rim], axis=1), "tmpl", axis=0, tiled=True)
    waves = jnp.pad(templates.reshape(rows, L), ((0, 0), (0, SPAN - L)))
    vmem = pl.BlockSpec(memory_space=pltpu.VMEM)
    out = pl.pallas_call(
        functools.partial(kernel, total, parts),
        out_shape=jax.ShapeDtypeStruct((total, time_dev), jnp.float32),
        in_specs=[pl.BlockSpec(memory_space=pltpu.SMEM)] + [vmem] * 5,
        out_specs=vmem,
        scratch_shapes=[
            pltpu.VMEM((rows * SLOTS, LANES), jnp.float32),
            pltpu.VMEM((window.shape[0] * SLOTS, LANES), jnp.float32),
            pltpu.VMEM((window.shape[0] * SLOTS, LANES), jnp.float32),
            pltpu.VMEM((total * SLOTS, LANES), jnp.float32),
            pltpu.VMEM((total * SLOTS, LANES), jnp.float32),
        ],
        compiler_params=pltpu.CompilerParams(vmem_limit_bytes=52 * 2**20),
    )(channels.reshape(rows), window, waves, moveouts.reshape(rows, 1), basis, inverse)
    return out.reshape(batches, count, time_dev)


def solution(mesh):
    placed = (
        P("tmpl", "tm"),
        P(None, "tmpl", None, None),
        P(None, "tmpl", None),
        P(None, "tmpl", None),
    )
    return jax.shard_map(
        per_device, mesh=mesh, in_specs=placed, out_specs=P(None, "tmpl", "tm"), check_vma=False
    )
```

```python
import functools
import math

import jax
import jax.numpy as jnp
import ml_dtypes
import numpy as np
from jax import lax
from jax.experimental import pallas as pl
from jax.experimental.pallas import tpu as pltpu
from jax.sharding import PartitionSpec as P

L = 200
LAGS = 56
SPAN = 256
LANES = 128
OUTER = 4
SLOTS = 8


class Gather:
    def __init__(self, win, send, recv, devices, windows, rows, time_dev):
        self.win, self.send, self.recv = win, send, recv
        self.rows, self.time_dev = rows, time_dev
        self.outer, self.inner = OUTER, devices // (2 * OUTER)
        me = lax.axis_index("tmpl")
        self.me, self.core = me, me % 2
        self.o, self.m = me // (2 * self.inner), me // 2 % self.inner
        self.tm, self.windows = lax.axis_index("tm"), windows
        self.turns = (0, 1, 3, 2)
        self.sent = []

    def index(self, k, j, core):
        o = (self.o - k + self.outer) % self.outer
        m = (self.m - j + self.inner) % self.inner
        return (o * self.inner + m) * 2 + core

    def block(self, k, j, core, first, columns):
        at = pl.multiple_of(self.index(k, j, core) * self.rows, self.rows)
        return self.win.at[pl.ds(at, self.rows), pl.ds(first, columns)]

    def copy(self, kind, k, j, ref, target):
        at = (kind * self.outer + k) * self.inner + j
        return pltpu.make_async_remote_copy(
            src_ref=ref,
            dst_ref=ref,
            send_sem=self.send.at[at],
            recv_sem=self.recv.at[at],
            device_id=target,
            device_id_type=pl.DeviceIdType.MESH,
        )

    def main(self, k, j):
        if j == 0:
            return self.copy(
                0, k, j, self.block(0, 0, self.core, 0, self.time_dev),
                (self.index(-k, 0, self.core), self.tm),
            )
        return self.copy(
            0, k, j, self.block(k, 0, self.core, 0, self.time_dev),
            (self.index(0, -j, self.core), self.tm),
        )

    def rim(self, k, j):
        ref = self.block(k, j, self.core, 0, SPAN)
        at = (self.outer + k) * self.inner + j
        return pltpu.make_async_remote_copy(
            src_ref=ref,
            dst_ref=self.block(k, j, self.core, self.time_dev, SPAN),
            send_sem=self.send.at[at],
            recv_sem=self.recv.at[at],
            device_id=(self.me, (self.tm + self.windows - 1) % self.windows),
            device_id_type=pl.DeviceIdType.MESH,
        )

    def across(self, k, j):
        return self.copy(
            2, k, j, self.block(k, j, self.core, 0, self.time_dev + SPAN),
            (self.index(0, 0, 1 - self.core), self.tm),
        )

    def go(self, copy):
        copy.start()
        self.sent.append(copy)

    def greet(self):
        barrier = pltpu.get_barrier_semaphore()
        peers = [(self.index(-k, 0, self.core), self.tm) for k in range(1, self.outer)]
        peers += [(self.index(0, -j, self.core), self.tm) for j in range(1, self.inner)]
        peers += [(self.index(0, 0, 1 - self.core), self.tm)]
        peers += [(self.me, (self.tm + 1) % self.windows)]
        for peer in peers:
            pl.semaphore_signal(
                barrier, inc=1, device_id=peer, device_id_type=pl.DeviceIdType.MESH
            )
        pl.semaphore_wait(barrier, len(peers))

    def own(self, records_ref):
        at = pl.multiple_of(self.me * self.rows, self.rows)
        self.win[pl.ds(at, self.rows), pl.ds(0, self.time_dev)] = records_ref[...]

    def run(self, beside=lambda: None):
        for k in self.turns[1:]:
            self.go(self.main(k, 0))
        for k in self.turns:
            if k:
                beside()
                self.main(k, 0).wait_recv()
            for j in range(1, self.inner):
                self.go(self.main(k, j))
            self.go(self.rim(k, 0))
        for j in range(1, self.inner):
            for k in self.turns:
                beside()
                self.main(k, j).wait_recv()
                self.go(self.rim(k, j))
        for j in range(self.inner):
            for k in self.turns:
                beside()
                self.rim(k, j).wait_recv()
                self.go(self.across(k, j))

    def finish(self):
        for j in range(self.inner):
            for k in self.turns:
                self.across(k, j).wait_recv()
        for copy in self.sent:
            copy.wait_send()

        @pl.when(self.tm == self.windows - 1)
        def _():
            rim = self.win.shape[0], SPAN
            self.win[:, pl.ds(self.time_dev, SPAN)] = jnp.zeros(rim, self.win.dtype)


def gather_kernel(devices, windows, records_ref, out_ref, win, send, recv):
    rows, time_dev = records_ref.shape
    moves = Gather(win, send, recv, devices, windows, rows, time_dev)
    moves.own(records_ref)
    moves.greet()
    moves.run()
    moves.finish()
    out_ref[...] = win[...]


def tables(count, freqs, width):
    turn = np.arange(count, dtype=np.int64)[:, None] * np.arange(freqs, dtype=np.int64)[None, :]
    angle = 2.0 * math.pi / width * (turn % width).astype(np.float64)
    return np.concatenate([np.cos(angle), np.sin(angle)], axis=1)


def spread(dst, first, rows, values, slots):
    for piece, slot in enumerate(slots):
        dst[pl.ds(first * SLOTS + slot, rows, stride=SLOTS), :] = values[
            :, piece * LANES : (piece + 1) * LANES
        ]


def waves_spectra(waves_ref, lags_ref, basis_ref, h_ref, rows):
    def step(i, carry):
        first = pl.multiple_of(i * rows, rows)
        wave = waves_ref[pl.ds(first, rows), :].astype(jnp.float32)
        lag = jnp.broadcast_to(lags_ref[pl.ds(first, rows), :], (rows, SPAN))
        bit = 1
        while bit < LAGS:
            wave = jnp.where((lag & bit) != 0, pltpu.roll(wave, bit, 1), wave)
            bit *= 2
        spec = jnp.dot(
            wave.astype(jnp.bfloat16), basis_ref[:SPAN, :], preferred_element_type=jnp.float32
        )
        spread(h_ref, first, rows, spec, (0, 1, 2, 4, 5, 6))
        return carry

    lax.fori_loop(0, waves_ref.shape[0] // rows, step, 0)


def record_spectra(window_ref, basis_ref, x_ref, y_ref, rows):
    def step(i, carry):
        first = pl.multiple_of(i * rows, rows)
        spec = jnp.dot(
            window_ref[pl.ds(first, rows), :], basis_ref[...], preferred_element_type=jnp.float32
        )
        spec = spec.astype(jnp.bfloat16).astype(jnp.float32)
        spread(x_ref, first, rows, spec, (0, 1, 2, 4, 5, 6))
        spread(y_ref, first, rows, spec, (4, 5, 6, 0, 1, 2))
        return carry

    lax.fori_loop(0, window_ref.shape[0] // rows, step, 0)


def correlate(chans_ref, h_ref, x_ref, y_ref, p_ref, q_ref, count, parts):
    def step(t, carry):
        same = [None] * 4
        cross = [None] * 4
        for k in range(parts):
            row = t * parts + k
            chan = pl.multiple_of(chans_ref[row] * SLOTS, SLOTS)
            h = h_ref[pl.ds(pl.multiple_of(row * SLOTS, SLOTS), SLOTS), :]
            a = h * x_ref[pl.ds(chan, SLOTS), :]
            b = h * y_ref[pl.ds(chan, SLOTS), :]
            lane = k % 4
            same[lane] = a if same[lane] is None else same[lane] + a
            cross[lane] = b if cross[lane] is None else cross[lane] + b
        at = pl.ds(pl.multiple_of(t * SLOTS, SLOTS), SLOTS)
        p_ref[at, :] = (same[0] + same[1]) + (same[2] + same[3])
        q_ref[at, :] = (cross[0] + cross[1]) + (cross[2] + cross[3])
        return carry

    lax.fori_loop(0, count, step, 0)


def back(p_ref, q_ref, inverse_ref, out_ref, count):
    real, imag = [], []
    for j in range(3):
        low, high = pl.ds(j, count, stride=SLOTS), pl.ds(j + 4, count, stride=SLOTS)
        real.append(p_ref[low, :] + p_ref[high, :])
        imag.append(q_ref[low, :] - q_ref[high, :])
    joint = jnp.concatenate(real + imag, axis=1)
    out_ref[...] = lax.dot_general(
        joint,
        inverse_ref[...],
        (((1,), (0,)), ((), ())),
        precision=lax.Precision.HIGHEST,
        preferred_element_type=jnp.float32,
    )


def kernel(
    count, parts, chans_ref, window_ref, waves_ref, lags_ref, basis_ref, inverse_ref, out_ref,
    h_ref, x_ref, y_ref, p_ref, q_ref,
):
    waves_spectra(waves_ref, lags_ref, basis_ref, h_ref, 256)
    record_spectra(window_ref, basis_ref, x_ref, y_ref, 256)
    correlate(chans_ref, h_ref, x_ref, y_ref, p_ref, q_ref, count, parts)
    back(p_ref, q_ref, inverse_ref, out_ref, count)


def per_device(records, templates, channels, moveouts):
    time_dev = records.shape[1]
    extra = L + LAGS - 2
    width = time_dev + extra
    freqs = width // 2 + 1
    wide = time_dev + SPAN
    batches, count, parts = channels.shape
    total = batches * count
    rows = total * parts
    forward = np.zeros((wide, 2 * freqs), np.float32)
    forward[:width] = tables(width, freqs, width)
    basis = jnp.asarray(forward.astype(ml_dtypes.bfloat16))
    freq = np.arange(freqs)
    weight = np.where((freq == 0) | (freq == freqs - 1), 1.0, 2.0) / width
    inverse = jnp.asarray(
        (tables(time_dev, freqs, width) * np.concatenate([weight, weight])).T.astype(np.float32)
    )
    devices, windows = lax.axis_size("tmpl"), lax.axis_size("tm")
    copies = 3 * devices // 2
    window = pl.pallas_call(
        functools.partial(gather_kernel, devices, windows),
        out_shape=jax.ShapeDtypeStruct((devices * records.shape[0], wide), records.dtype),
        in_specs=[pl.BlockSpec(memory_space=pltpu.VMEM)],
        out_specs=pl.BlockSpec(memory_space=pltpu.VMEM),
        scratch_shapes=[
            pltpu.VMEM((devices * records.shape[0], wide), records.dtype),
            pltpu.SemaphoreType.DMA((copies,)),
            pltpu.SemaphoreType.DMA((copies,)),
        ],
        compiler_params=pltpu.CompilerParams(
            collective_id=0, has_side_effects=True, vmem_limit_bytes=24 * 2**20
        ),
    )(records)
    waves = jnp.pad(templates.reshape(rows, L), ((0, 0), (0, SPAN - L)))
    vmem = pl.BlockSpec(memory_space=pltpu.VMEM)
    out = pl.pallas_call(
        functools.partial(kernel, total, parts),
        out_shape=jax.ShapeDtypeStruct((total, time_dev), jnp.float32),
        in_specs=[pl.BlockSpec(memory_space=pltpu.SMEM)] + [vmem] * 5,
        out_specs=vmem,
        scratch_shapes=[
            pltpu.VMEM((rows * SLOTS, LANES), jnp.float32),
            pltpu.VMEM((window.shape[0] * SLOTS, LANES), jnp.float32),
            pltpu.VMEM((window.shape[0] * SLOTS, LANES), jnp.float32),
            pltpu.VMEM((total * SLOTS, LANES), jnp.float32),
            pltpu.VMEM((total * SLOTS, LANES), jnp.float32),
        ],
        compiler_params=pltpu.CompilerParams(vmem_limit_bytes=52 * 2**20),
    )(channels.reshape(rows), window, waves, moveouts.reshape(rows, 1), basis, inverse)
    return out.reshape(batches, count, time_dev)


def solution(mesh):
    placed = (
        P("tmpl", "tm"),
        P(None, "tmpl", None, None),
        P(None, "tmpl", None),
        P(None, "tmpl", None),
    )
    return jax.shard_map(
        per_device, mesh=mesh, in_specs=placed, out_specs=P(None, "tmpl", "tm"), check_vma=False
    )
```

```python
import functools
import math

import jax
import jax.numpy as jnp
import ml_dtypes
import numpy as np
from jax import lax
from jax.experimental import pallas as pl
from jax.experimental.pallas import tpu as pltpu
from jax.sharding import PartitionSpec as P

L = 200
LAGS = 56
SPAN = 256
LANES = 128
OUTER = 4
CHUNK = 4
SLOTS = 8


class Gather:
    def __init__(self, win, send, recv, devices, windows, rows, time_dev):
        self.win, self.send, self.recv = win, send, recv
        self.rows, self.time_dev = rows, time_dev
        self.outer, self.inner = OUTER, devices // (2 * OUTER)
        me = lax.axis_index("tmpl")
        self.me, self.core = me, me % 2
        self.o, self.m = me // (2 * self.inner), me // 2 % self.inner
        self.tm, self.windows = lax.axis_index("tm"), windows
        self.turns = (0, 1, 3, 2)
        self.sent = []

    def index(self, k, j, core):
        o = (self.o - k + self.outer) % self.outer
        m = (self.m - j + self.inner) % self.inner
        return (o * self.inner + m) * 2 + core

    def block(self, k, j, core, first, columns):
        at = pl.multiple_of(self.index(k, j, core) * self.rows, self.rows)
        return self.win.at[pl.ds(at, self.rows), pl.ds(first, columns)]

    def copy(self, kind, k, j, ref, target):
        at = (kind * self.outer + k) * self.inner + j
        return pltpu.make_async_remote_copy(
            src_ref=ref,
            dst_ref=ref,
            send_sem=self.send.at[at],
            recv_sem=self.recv.at[at],
            device_id=target,
            device_id_type=pl.DeviceIdType.MESH,
        )

    def main(self, k, j):
        if j == 0:
            return self.copy(
                0, k, j, self.block(0, 0, self.core, 0, self.time_dev),
                (self.index(-k, 0, self.core), self.tm),
            )
        return self.copy(
            0, k, j, self.block(k, 0, self.core, 0, self.time_dev),
            (self.index(0, -j, self.core), self.tm),
        )

    def rim(self, k, j):
        ref = self.block(k, j, self.core, 0, SPAN)
        at = (self.outer + k) * self.inner + j
        return pltpu.make_async_remote_copy(
            src_ref=ref,
            dst_ref=self.block(k, j, self.core, self.time_dev, SPAN),
            send_sem=self.send.at[at],
            recv_sem=self.recv.at[at],
            device_id=(self.me, (self.tm + self.windows - 1) % self.windows),
            device_id_type=pl.DeviceIdType.MESH,
        )

    def across(self, k, j):
        return self.copy(
            2, k, j, self.block(k, j, self.core, 0, self.time_dev + SPAN),
            (self.index(0, 0, 1 - self.core), self.tm),
        )

    def go(self, copy):
        copy.start()
        self.sent.append(copy)

    def greet(self):
        barrier = pltpu.get_barrier_semaphore()
        peers = [(self.index(-k, 0, self.core), self.tm) for k in range(1, self.outer)]
        peers += [(self.index(0, -j, self.core), self.tm) for j in range(1, self.inner)]
        peers += [(self.index(0, 0, 1 - self.core), self.tm)]
        peers += [(self.me, (self.tm + 1) % self.windows)]
        for peer in peers:
            pl.semaphore_signal(
                barrier, inc=1, device_id=peer, device_id_type=pl.DeviceIdType.MESH
            )
        pl.semaphore_wait(barrier, len(peers))

    def own(self, records_ref):
        at = pl.multiple_of(self.me * self.rows, self.rows)
        self.win[pl.ds(at, self.rows), pl.ds(0, self.time_dev)] = records_ref[...]

    def run(self, beside=lambda: None):
        for k in self.turns[1:]:
            self.go(self.main(k, 0))
        for k in self.turns:
            if k:
                beside()
                self.main(k, 0).wait_recv()
            for j in range(1, self.inner):
                self.go(self.main(k, j))
            self.go(self.rim(k, 0))
        for j in range(1, self.inner):
            for k in self.turns:
                beside()
                self.main(k, j).wait_recv()
                self.go(self.rim(k, j))
        for j in range(self.inner):
            for k in self.turns:
                beside()
                self.rim(k, j).wait_recv()
                self.go(self.across(k, j))

    def finish(self):
        for j in range(self.inner):
            for k in self.turns:
                self.across(k, j).wait_recv()
        for copy in self.sent:
            copy.wait_send()

        @pl.when(self.tm == self.windows - 1)
        def _():
            rim = self.win.shape[0], SPAN
            self.win[:, pl.ds(self.time_dev, SPAN)] = jnp.zeros(rim, self.win.dtype)


def tables(count, freqs, width):
    turn = np.arange(count, dtype=np.int64)[:, None] * np.arange(freqs, dtype=np.int64)[None, :]
    angle = 2.0 * math.pi / width * (turn % width).astype(np.float64)
    return np.concatenate([np.cos(angle), np.sin(angle)], axis=1)


def spread(dst, first, rows, values, slots):
    for piece, slot in enumerate(slots):
        dst[pl.ds(first * SLOTS + slot, rows, stride=SLOTS), :] = values[
            :, piece * LANES : (piece + 1) * LANES
        ]


def waves_spectra(waves_ref, lags_ref, basis_ref, h_ref, parts, chunk):
    rows = CHUNK * parts
    first = chunk * rows
    wave = waves_ref[pl.ds(first, rows), :].astype(jnp.float32)
    wave = jnp.concatenate([wave, jnp.zeros((rows, SPAN - L), jnp.float32)], axis=1)
    square = (parts, parts)
    eye = lax.broadcasted_iota(jnp.int32, square, 0) == lax.broadcasted_iota(jnp.int32, square, 1)
    lags = []
    for t in range(chunk * CHUNK, (chunk + 1) * CHUNK):
        across = jnp.broadcast_to(lags_ref[pl.ds(t, 1), :].astype(jnp.float32), square)
        lags.append(jnp.sum(jnp.where(eye, across, 0.0), axis=1, keepdims=True))
    lag = jnp.broadcast_to(jnp.concatenate(lags, axis=0).astype(jnp.int32), (rows, SPAN))
    bit = 1
    while bit < LAGS:
        wave = jnp.where((lag & bit) != 0, pltpu.roll(wave, bit, 1), wave)
        bit *= 2
    spec = jnp.dot(
        wave.astype(jnp.bfloat16), basis_ref[:SPAN, :], preferred_element_type=jnp.float32
    )
    spread(h_ref, first, rows, spec, (0, 1, 2, 4, 5, 6))


def record_spectra(window_ref, basis_ref, x_ref, y_ref, rows):
    def step(i, carry):
        first = pl.multiple_of(i * rows, rows)
        spec = jnp.dot(
            window_ref[pl.ds(first, rows), :], basis_ref[...], preferred_element_type=jnp.float32
        )
        spec = spec.astype(jnp.bfloat16).astype(jnp.float32)
        spread(x_ref, first, rows, spec, (0, 1, 2, 4, 5, 6))
        spread(y_ref, first, rows, spec, (4, 5, 6, 0, 1, 2))
        return carry

    lax.fori_loop(0, window_ref.shape[0] // rows, step, 0)


def correlate(chans_ref, h_ref, x_ref, y_ref, p_ref, q_ref, count, parts):
    def step(t, carry):
        same = [None] * 4
        cross = [None] * 4
        for k in range(parts):
            row = t * parts + k
            chan = chans_ref[t, k] * SLOTS
            h = h_ref[pl.ds(pl.multiple_of(row * SLOTS, SLOTS), SLOTS), :]
            a = h * x_ref[pl.ds(chan, SLOTS), :]
            b = h * y_ref[pl.ds(chan, SLOTS), :]
            lane = k % 4
            same[lane] = a if same[lane] is None else same[lane] + a
            cross[lane] = b if cross[lane] is None else cross[lane] + b
        at = pl.ds(pl.multiple_of(t * SLOTS, SLOTS), SLOTS)
        p_ref[at, :] = (same[0] + same[1]) + (same[2] + same[3])
        q_ref[at, :] = (cross[0] + cross[1]) + (cross[2] + cross[3])
        return carry

    lax.fori_loop(0, count, step, 0)


def back(p_ref, q_ref, inverse_ref, out_ref, count):
    real, imag = [], []
    for j in range(3):
        low, high = pl.ds(j, count, stride=SLOTS), pl.ds(j + 4, count, stride=SLOTS)
        real.append(p_ref[low, :] + p_ref[high, :])
        imag.append(q_ref[low, :] - q_ref[high, :])
    joint = jnp.concatenate(real + imag, axis=1)
    out_ref[...] = lax.dot_general(
        joint,
        inverse_ref[...],
        (((1,), (0,)), ((), ())),
        precision=lax.Precision.HIGHEST,
        preferred_element_type=jnp.float32,
    )


def kernel(
    devices, windows, chans_ref, records_ref, waves_ref, lags_ref, basis_ref, inverse_ref, out_ref,
    win, send, recv, h_ref, x_ref, y_ref, p_ref, q_ref,
):
    count, parts = chans_ref.shape
    rows, time_dev = records_ref.shape
    moves = Gather(win, send, recv, devices, windows, rows, time_dev)
    chunks = list(range(count // CHUNK))

    def beside():
        if chunks:
            waves_spectra(waves_ref, lags_ref, basis_ref, h_ref, parts, chunks.pop(0))

    moves.own(records_ref)
    moves.greet()
    moves.run(beside)
    while chunks:
        beside()
    moves.finish()
    record_spectra(win, basis_ref, x_ref, y_ref, 256)
    correlate(chans_ref, h_ref, x_ref, y_ref, p_ref, q_ref, count, parts)
    back(p_ref, q_ref, inverse_ref, out_ref, count)


def per_device(records, templates, channels, moveouts):
    time_dev = records.shape[1]
    extra = L + LAGS - 2
    width = time_dev + extra
    freqs = width // 2 + 1
    wide = time_dev + SPAN
    batches, count, parts = channels.shape
    total = batches * count
    rows = total * parts
    forward = np.zeros((wide, 2 * freqs), np.float32)
    forward[:width] = tables(width, freqs, width)
    basis = jnp.asarray(forward.astype(ml_dtypes.bfloat16))
    freq = np.arange(freqs)
    weight = np.where((freq == 0) | (freq == freqs - 1), 1.0, 2.0) / width
    inverse = jnp.asarray(
        (tables(time_dev, freqs, width) * np.concatenate([weight, weight])).T.astype(np.float32)
    )
    devices, windows = lax.axis_size("tmpl"), lax.axis_size("tm")
    copies = 3 * devices // 2
    everyone = devices * records.shape[0]
    vmem = pl.BlockSpec(memory_space=pltpu.VMEM)
    out = pl.pallas_call(
        functools.partial(kernel, devices, windows),
        out_shape=jax.ShapeDtypeStruct((total, time_dev), jnp.float32),
        in_specs=[pl.BlockSpec(memory_space=pltpu.SMEM)] + [vmem] * 5,
        out_specs=vmem,
        scratch_shapes=[
            pltpu.VMEM((everyone, wide), records.dtype),
            pltpu.SemaphoreType.DMA((copies,)),
            pltpu.SemaphoreType.DMA((copies,)),
            pltpu.VMEM((rows * SLOTS, LANES), jnp.float32),
            pltpu.VMEM((everyone * SLOTS, LANES), jnp.float32),
            pltpu.VMEM((everyone * SLOTS, LANES), jnp.float32),
            pltpu.VMEM((total * SLOTS, LANES), jnp.float32),
            pltpu.VMEM((total * SLOTS, LANES), jnp.float32),
        ],
        compiler_params=pltpu.CompilerParams(
            collective_id=0, has_side_effects=True, vmem_limit_bytes=52 * 2**20
        ),
    )(
        channels.reshape(total, parts),
        records,
        templates.reshape(rows, L),
        moveouts.reshape(total, parts),
        basis,
        inverse,
    )
    return out.reshape(batches, count, time_dev)


def solution(mesh):
    placed = (
        P("tmpl", "tm"),
        P(None, "tmpl", None, None),
        P(None, "tmpl", None),
        P(None, "tmpl", None),
    )
    return jax.shard_map(
        per_device, mesh=mesh, in_specs=placed, out_specs=P(None, "tmpl", "tm"), check_vma=False
    )
```

```python
import functools
import math

import jax
import jax.numpy as jnp
import ml_dtypes
import numpy as np
from jax import lax
from jax.experimental import pallas as pl
from jax.experimental.pallas import tpu as pltpu
from jax.sharding import PartitionSpec as P

L = 200
LAGS = 56
SPAN = 256
LANES = 128
OUTER = 4
CHUNK = 4
SLOTS = 8


class Gather:
    def __init__(self, win, send, recv, devices, windows, rows, time_dev):
        self.win, self.send, self.recv = win, send, recv
        self.rows, self.time_dev = rows, time_dev
        self.outer, self.inner = OUTER, devices // (2 * OUTER)
        me = lax.axis_index("tmpl")
        self.me, self.core = me, me % 2
        self.o, self.m = me // (2 * self.inner), me // 2 % self.inner
        self.tm, self.windows = lax.axis_index("tm"), windows
        self.turns = (0, 1, 3, 2)
        self.sent = []

    def index(self, k, j, core):
        o = (self.o - k + self.outer) % self.outer
        m = (self.m - j + self.inner) % self.inner
        return (o * self.inner + m) * 2 + core

    def block(self, k, j, core, first, columns):
        at = pl.multiple_of(self.index(k, j, core) * self.rows, self.rows)
        return self.win.at[pl.ds(at, self.rows), pl.ds(first, columns)]

    def copy(self, kind, k, j, ref, target):
        at = (kind * self.outer + k) * self.inner + j
        return pltpu.make_async_remote_copy(
            src_ref=ref,
            dst_ref=ref,
            send_sem=self.send.at[at],
            recv_sem=self.recv.at[at],
            device_id=target,
            device_id_type=pl.DeviceIdType.MESH,
        )

    def main(self, k, j):
        if j == 0:
            return self.copy(
                0, k, j, self.block(0, 0, self.core, 0, self.time_dev),
                (self.index(-k, 0, self.core), self.tm),
            )
        return self.copy(
            0, k, j, self.block(k, 0, self.core, 0, self.time_dev),
            (self.index(0, -j, self.core), self.tm),
        )

    def rim(self, k, j):
        ref = self.block(k, j, self.core, 0, SPAN)
        at = (self.outer + k) * self.inner + j
        return pltpu.make_async_remote_copy(
            src_ref=ref,
            dst_ref=self.block(k, j, self.core, self.time_dev, SPAN),
            send_sem=self.send.at[at],
            recv_sem=self.recv.at[at],
            device_id=(self.me, (self.tm + self.windows - 1) % self.windows),
            device_id_type=pl.DeviceIdType.MESH,
        )

    def across(self, k, j):
        return self.copy(
            2, k, j, self.block(k, j, self.core, 0, self.time_dev + SPAN),
            (self.index(0, 0, 1 - self.core), self.tm),
        )

    def go(self, copy):
        copy.start()
        self.sent.append(copy)

    def greet(self):
        barrier = pltpu.get_barrier_semaphore()
        peers = [(self.index(-k, 0, self.core), self.tm) for k in range(1, self.outer)]
        peers += [(self.index(0, -j, self.core), self.tm) for j in range(1, self.inner)]
        peers += [(self.index(0, 0, 1 - self.core), self.tm)]
        peers += [(self.me, (self.tm + 1) % self.windows)]
        for peer in peers:
            pl.semaphore_signal(
                barrier, inc=1, device_id=peer, device_id_type=pl.DeviceIdType.MESH
            )
        pl.semaphore_wait(barrier, len(peers))

    def own(self, records_ref):
        at = pl.multiple_of(self.me * self.rows, self.rows)
        self.win[pl.ds(at, self.rows), pl.ds(0, self.time_dev)] = records_ref[...]

    def run(self, beside, complete):
        for k in self.turns[1:]:
            self.go(self.main(k, 0))
        for k in self.turns:
            if k:
                beside()
                self.main(k, 0).wait_recv()
            for j in range(1, self.inner):
                self.go(self.main(k, j))
            self.go(self.rim(k, 0))
        for j in range(1, self.inner):
            for k in self.turns:
                beside()
                self.main(k, j).wait_recv()
                self.go(self.rim(k, j))
        for j in range(self.inner):
            for k in self.turns:
                beside()
                self.rim(k, j).wait_recv()
                self.go(self.across(k, j))
                complete(self.index(k, j, self.core))

    def finish(self, complete):
        for j in range(self.inner):
            for k in self.turns:
                self.across(k, j).wait_recv()
                complete(self.index(k, j, 1 - self.core))
        for copy in self.sent:
            copy.wait_send()


def tables(count, freqs, width):
    turn = np.arange(count, dtype=np.int64)[:, None] * np.arange(freqs, dtype=np.int64)[None, :]
    angle = 2.0 * math.pi / width * (turn % width).astype(np.float64)
    return np.concatenate([np.cos(angle), np.sin(angle)], axis=1)


def spread(dst, first, rows, values, slots):
    for piece, slot in enumerate(slots):
        dst[pl.ds(first * SLOTS + slot, rows, stride=SLOTS), :] = values[
            :, piece * LANES : (piece + 1) * LANES
        ]


def waves_spectra(waves_ref, lags_ref, basis_ref, h_ref, parts, chunk):
    rows = CHUNK * parts
    first = chunk * rows
    wave = waves_ref[pl.ds(first, rows), :].astype(jnp.float32)
    wave = jnp.concatenate([wave, jnp.zeros((rows, SPAN - L), jnp.float32)], axis=1)
    square = (parts, parts)
    eye = lax.broadcasted_iota(jnp.int32, square, 0) == lax.broadcasted_iota(jnp.int32, square, 1)
    lags = []
    for t in range(chunk * CHUNK, (chunk + 1) * CHUNK):
        across = jnp.broadcast_to(lags_ref[pl.ds(t, 1), :].astype(jnp.float32), square)
        lags.append(jnp.sum(jnp.where(eye, across, 0.0), axis=1, keepdims=True))
    lag = jnp.broadcast_to(jnp.concatenate(lags, axis=0).astype(jnp.int32), (rows, SPAN))
    bit = 1
    while bit < LAGS:
        wave = jnp.where((lag & bit) != 0, pltpu.roll(wave, bit, 1), wave)
        bit *= 2
    spec = jnp.dot(
        wave.astype(jnp.bfloat16), basis_ref[:SPAN, :], preferred_element_type=jnp.float32
    )
    spread(h_ref, first, rows, spec, (0, 1, 2, 4, 5, 6))


def record_spectra(win, first, rows, time_dev, keep, basis_ref, x_ref, y_ref):
    at = pl.ds(first, rows)
    spec = jnp.dot(
        win[at, :time_dev], basis_ref[:time_dev, :], preferred_element_type=jnp.float32
    )
    spec += keep * jnp.dot(
        win[at, time_dev:], basis_ref[time_dev:, :], preferred_element_type=jnp.float32
    )
    spec = spec.astype(jnp.bfloat16).astype(jnp.float32)
    spread(x_ref, first, rows, spec, (0, 1, 2, 4, 5, 6))
    spread(y_ref, first, rows, spec, (4, 5, 6, 0, 1, 2))


def correlate(chans_ref, h_ref, x_ref, y_ref, p_ref, q_ref, count, parts):
    def step(t, carry):
        same = [None] * 4
        cross = [None] * 4
        for k in range(parts):
            row = t * parts + k
            chan = chans_ref[t, k] * SLOTS
            h = h_ref[pl.ds(pl.multiple_of(row * SLOTS, SLOTS), SLOTS), :]
            a = h * x_ref[pl.ds(chan, SLOTS), :]
            b = h * y_ref[pl.ds(chan, SLOTS), :]
            lane = k % 4
            same[lane] = a if same[lane] is None else same[lane] + a
            cross[lane] = b if cross[lane] is None else cross[lane] + b
        at = pl.ds(pl.multiple_of(t * SLOTS, SLOTS), SLOTS)
        p_ref[at, :] = (same[0] + same[1]) + (same[2] + same[3])
        q_ref[at, :] = (cross[0] + cross[1]) + (cross[2] + cross[3])
        return carry

    lax.fori_loop(0, count, step, 0)


def back(p_ref, q_ref, inverse_ref, out_ref, count):
    real, imag = [], []
    for j in range(3):
        low, high = pl.ds(j, count, stride=SLOTS), pl.ds(j + 4, count, stride=SLOTS)
        real.append(p_ref[low, :] + p_ref[high, :])
        imag.append(q_ref[low, :] - q_ref[high, :])
    joint = jnp.concatenate(real + imag, axis=1)
    out_ref[...] = lax.dot_general(
        joint,
        inverse_ref[...],
        (((1,), (0,)), ((), ())),
        precision=lax.Precision.HIGHEST,
        preferred_element_type=jnp.float32,
    )


def kernel(
    devices, windows, chans_ref, records_ref, waves_ref, lags_ref, basis_ref, inverse_ref, out_ref,
    win, send, recv, h_ref, x_ref, y_ref, p_ref, q_ref,
):
    count, parts = chans_ref.shape
    rows, time_dev = records_ref.shape
    moves = Gather(win, send, recv, devices, windows, rows, time_dev)
    chunks = list(range(count // CHUNK))

    def beside():
        if chunks:
            waves_spectra(waves_ref, lags_ref, basis_ref, h_ref, parts, chunks.pop(0))

    keep = jnp.where(moves.tm == windows - 1, 0.0, 1.0).astype(jnp.float32)

    def complete(index):
        first = pl.multiple_of(index * rows, rows)
        record_spectra(win, first, rows, time_dev, keep, basis_ref, x_ref, y_ref)

    moves.own(records_ref)
    moves.greet()
    moves.run(beside, complete)
    while chunks:
        beside()
    moves.finish(complete)
    correlate(chans_ref, h_ref, x_ref, y_ref, p_ref, q_ref, count, parts)
    back(p_ref, q_ref, inverse_ref, out_ref, count)


def per_device(records, templates, channels, moveouts):
    time_dev = records.shape[1]
    extra = L + LAGS - 2
    width = time_dev + extra
    freqs = width // 2 + 1
    wide = time_dev + SPAN
    batches, count, parts = channels.shape
    total = batches * count
    rows = total * parts
    forward = np.zeros((wide, 2 * freqs), np.float32)
    forward[:width] = tables(width, freqs, width)
    basis = jnp.asarray(forward.astype(ml_dtypes.bfloat16))
    freq = np.arange(freqs)
    weight = np.where((freq == 0) | (freq == freqs - 1), 1.0, 2.0) / width
    inverse = jnp.asarray(
        (tables(time_dev, freqs, width) * np.concatenate([weight, weight])).T.astype(np.float32)
    )
    devices, windows = lax.axis_size("tmpl"), lax.axis_size("tm")
    copies = 3 * devices // 2
    everyone = devices * records.shape[0]
    vmem = pl.BlockSpec(memory_space=pltpu.VMEM)
    out = pl.pallas_call(
        functools.partial(kernel, devices, windows),
        out_shape=jax.ShapeDtypeStruct((total, time_dev), jnp.float32),
        in_specs=[pl.BlockSpec(memory_space=pltpu.SMEM)] + [vmem] * 5,
        out_specs=vmem,
        scratch_shapes=[
            pltpu.VMEM((everyone, wide), records.dtype),
            pltpu.SemaphoreType.DMA((copies,)),
            pltpu.SemaphoreType.DMA((copies,)),
            pltpu.VMEM((rows * SLOTS, LANES), jnp.float32),
            pltpu.VMEM((everyone * SLOTS, LANES), jnp.float32),
            pltpu.VMEM((everyone * SLOTS, LANES), jnp.float32),
            pltpu.VMEM((total * SLOTS, LANES), jnp.float32),
            pltpu.VMEM((total * SLOTS, LANES), jnp.float32),
        ],
        compiler_params=pltpu.CompilerParams(
            collective_id=0, has_side_effects=True, vmem_limit_bytes=52 * 2**20
        ),
    )(
        channels.reshape(total, parts),
        records,
        templates.reshape(rows, L),
        moveouts.reshape(total, parts),
        basis,
        inverse,
    )
    return out.reshape(batches, count, time_dev)


def solution(mesh):
    placed = (
        P("tmpl", "tm"),
        P(None, "tmpl", None, None),
        P(None, "tmpl", None),
        P(None, "tmpl", None),
    )
    return jax.shard_map(
        per_device, mesh=mesh, in_specs=placed, out_specs=P(None, "tmpl", "tm"), check_vma=False
    )
```

```python
import functools
import math

import jax
import jax.numpy as jnp
import ml_dtypes
import numpy as np
from jax import lax
from jax.experimental import pallas as pl
from jax.experimental.pallas import tpu as pltpu
from jax.sharding import PartitionSpec as P

L = 200
LAGS = 56
SPAN = 256
LANES = 128
OUTER = 4
CHUNK = 4
SLOTS = 8


class Gather:
    def __init__(self, win, send, recv, devices, windows, rows, time_dev):
        self.win, self.send, self.recv = win, send, recv
        self.rows, self.time_dev = rows, time_dev
        self.outer, self.inner = OUTER, devices // (2 * OUTER)
        me = lax.axis_index("tmpl")
        self.me, self.core = me, me % 2
        self.o, self.m = me // (2 * self.inner), me // 2 % self.inner
        self.tm, self.windows = lax.axis_index("tm"), windows
        self.turns = (0, 1, 3, 2)
        self.sent = []

    def index(self, k, j, core):
        o = (self.o - k + self.outer) % self.outer
        m = (self.m - j + self.inner) % self.inner
        return (o * self.inner + m) * 2 + core

    def block(self, k, j, core, first, columns):
        at = pl.multiple_of(self.index(k, j, core) * self.rows, self.rows)
        return self.win.at[pl.ds(at, self.rows), pl.ds(first, columns)]

    def copy(self, kind, k, j, ref, target):
        at = (kind * self.outer + k) * self.inner + j
        return pltpu.make_async_remote_copy(
            src_ref=ref,
            dst_ref=ref,
            send_sem=self.send.at[at],
            recv_sem=self.recv.at[at],
            device_id=target,
            device_id_type=pl.DeviceIdType.MESH,
        )

    def main(self, k, j):
        if j == 0:
            return self.copy(
                0, k, j, self.block(0, 0, self.core, 0, self.time_dev),
                (self.index(-k, 0, self.core), self.tm),
            )
        return self.copy(
            0, k, j, self.block(k, 0, self.core, 0, self.time_dev),
            (self.index(0, -j, self.core), self.tm),
        )

    def rim(self, k, j):
        ref = self.block(k, j, self.core, 0, SPAN)
        at = (self.outer + k) * self.inner + j
        return pltpu.make_async_remote_copy(
            src_ref=ref,
            dst_ref=self.block(k, j, self.core, self.time_dev, SPAN),
            send_sem=self.send.at[at],
            recv_sem=self.recv.at[at],
            device_id=(self.me, (self.tm + self.windows - 1) % self.windows),
            device_id_type=pl.DeviceIdType.MESH,
        )

    def across(self, k, j):
        return self.copy(
            2, k, j, self.block(k, j, self.core, 0, self.time_dev + SPAN),
            (self.index(0, 0, 1 - self.core), self.tm),
        )

    def go(self, copy):
        copy.start()
        self.sent.append(copy)

    def greet(self):
        barrier = pltpu.get_barrier_semaphore()
        peers = [(self.index(-k, 0, self.core), self.tm) for k in range(1, self.outer)]
        peers += [(self.index(0, -j, self.core), self.tm) for j in range(1, self.inner)]
        peers += [(self.index(0, 0, 1 - self.core), self.tm)]
        peers += [(self.me, (self.tm + 1) % self.windows)]
        for peer in peers:
            pl.semaphore_signal(
                barrier, inc=1, device_id=peer, device_id_type=pl.DeviceIdType.MESH
            )
        pl.semaphore_wait(barrier, len(peers))

    def own(self, records_ref):
        at = pl.multiple_of(self.me * self.rows, self.rows)
        self.win[pl.ds(at, self.rows), pl.ds(0, self.time_dev)] = records_ref[...]

    def run(self, beside, complete):
        for k in self.turns[1:]:
            self.go(self.main(k, 0))
        for k in self.turns:
            if k:
                beside()
                self.main(k, 0).wait_recv()
            for j in range(1, self.inner):
                self.go(self.main(k, j))
            self.go(self.rim(k, 0))
        for j in range(1, self.inner):
            for k in self.turns:
                beside()
                self.main(k, j).wait_recv()
                self.go(self.rim(k, j))
        for j in range(self.inner):
            for k in self.turns:
                beside()
                self.rim(k, j).wait_recv()
                self.go(self.across(k, j))
                complete(self.index(k, j, self.core))

    def finish(self, complete):
        for j in range(self.inner):
            for k in self.turns:
                self.across(k, j).wait_recv()
                complete(self.index(k, j, 1 - self.core))
        for copy in self.sent:
            copy.wait_send()


def tables(count, freqs, width):
    turn = np.arange(count, dtype=np.int64)[:, None] * np.arange(freqs, dtype=np.int64)[None, :]
    angle = 2.0 * math.pi / width * (turn % width).astype(np.float64)
    return np.concatenate([np.cos(angle), np.sin(angle)], axis=1)


def spread(dst, first, rows, values, slots):
    for piece, slot in enumerate(slots):
        dst[pl.ds(first * SLOTS + slot, rows, stride=SLOTS), :] = values[
            :, piece * LANES : (piece + 1) * LANES
        ]


def waves_spectra(waves_ref, lags_ref, basis_ref, h_ref, parts, chunk):
    rows = CHUNK * parts
    first = chunk * rows
    wave = waves_ref[pl.ds(first, rows), :].astype(jnp.float32)
    wave = jnp.concatenate([wave, jnp.zeros((rows, SPAN - L), jnp.float32)], axis=1)
    square = (parts, parts)
    eye = lax.broadcasted_iota(jnp.int32, square, 0) == lax.broadcasted_iota(jnp.int32, square, 1)
    lags = []
    for t in range(chunk * CHUNK, (chunk + 1) * CHUNK):
        across = jnp.broadcast_to(lags_ref[pl.ds(t, 1), :].astype(jnp.float32), square)
        lags.append(jnp.sum(jnp.where(eye, across, 0.0), axis=1, keepdims=True))
    lag = jnp.broadcast_to(jnp.concatenate(lags, axis=0).astype(jnp.int32), (rows, SPAN))
    bit = 1
    while bit < LAGS:
        wave = jnp.where((lag & bit) != 0, pltpu.roll(wave, bit, 1), wave)
        bit *= 2
    spec = jnp.dot(
        wave.astype(jnp.bfloat16), basis_ref[:SPAN, :], preferred_element_type=jnp.float32
    )
    spread(h_ref, first, rows, spec, (0, 1, 2, 4, 5, 6))


def record_spectra(win, first, rows, time_dev, keep, basis_ref, x_ref, y_ref):
    at = pl.ds(first, rows)
    spec = jnp.dot(
        win[at, :time_dev], basis_ref[:time_dev, :], preferred_element_type=jnp.float32
    )
    spec += keep * jnp.dot(
        win[at, time_dev:], basis_ref[time_dev:, :], preferred_element_type=jnp.float32
    )
    spec = spec.astype(jnp.bfloat16).astype(jnp.float32)
    spread(x_ref, first, rows, spec, (0, 1, 2, 4, 5, 6))
    spread(y_ref, first, rows, spec, (4, 5, 6, 0, 1, 2))


def correlate(chans_ref, h_ref, x_ref, y_ref, p_ref, q_ref, count, parts):
    def step(t, carry):
        same = [None] * 4
        cross = [None] * 4
        for k in range(parts):
            row = t * parts + k
            chan = chans_ref[t, k] * SLOTS
            h = h_ref[pl.ds(pl.multiple_of(row * SLOTS, SLOTS), SLOTS), :]
            a = h * x_ref[pl.ds(chan, SLOTS), :]
            b = h * y_ref[pl.ds(chan, SLOTS), :]
            lane = k % 4
            same[lane] = a if same[lane] is None else same[lane] + a
            cross[lane] = b if cross[lane] is None else cross[lane] + b
        at = pl.ds(pl.multiple_of(t * SLOTS, SLOTS), SLOTS)
        p_ref[at, :] = (same[0] + same[1]) + (same[2] + same[3])
        q_ref[at, :] = (cross[0] + cross[1]) + (cross[2] + cross[3])
        return carry

    lax.fori_loop(0, count, step, 0)


def back(p_ref, q_ref, inverse_ref, out_ref, count):
    real, imag = [], []
    for j in range(3):
        low, high = pl.ds(j, count, stride=SLOTS), pl.ds(j + 4, count, stride=SLOTS)
        real.append(p_ref[low, :] + p_ref[high, :])
        imag.append(q_ref[low, :] - q_ref[high, :])
    joint = jnp.concatenate(real + imag, axis=1)
    out_ref[...] = lax.dot_general(
        joint,
        inverse_ref[...],
        (((1,), (0,)), ((), ())),
        precision=lax.Precision.HIGHEST,
        preferred_element_type=jnp.float32,
    )


def kernel(
    devices, windows, chans_ref, records_ref, lags_ref, waves_far, basis_far, inverse_far, out_ref,
    waves_ref, basis_ref, inverse_ref, load, win, send, recv, h_ref, x_ref, y_ref, p_ref, q_ref,
):
    count, parts = chans_ref.shape
    rows, time_dev = records_ref.shape
    moves = Gather(win, send, recv, devices, windows, rows, time_dev)
    chunks = list(range(count // CHUNK))

    pairs = ((waves_far, waves_ref), (basis_far, basis_ref), (inverse_far, inverse_ref))
    loads = [pltpu.make_async_copy(a, b, load.at[i]) for i, (a, b) in enumerate(pairs)]
    for copy in loads:
        copy.start()
    pending = loads[:2]

    def beside():
        while pending:
            pending.pop(0).wait()
        if chunks:
            waves_spectra(waves_ref, lags_ref, basis_ref, h_ref, parts, chunks.pop(0))

    keep = jnp.where(moves.tm == windows - 1, 0.0, 1.0).astype(jnp.float32)

    def complete(index):
        first = pl.multiple_of(index * rows, rows)
        record_spectra(win, first, rows, time_dev, keep, basis_ref, x_ref, y_ref)

    moves.own(records_ref)
    moves.greet()
    moves.run(beside, complete)
    while chunks:
        beside()
    moves.finish(complete)
    correlate(chans_ref, h_ref, x_ref, y_ref, p_ref, q_ref, count, parts)
    loads[2].wait()
    back(p_ref, q_ref, inverse_ref, out_ref, count)


def per_device(records, templates, channels, moveouts):
    time_dev = records.shape[1]
    extra = L + LAGS - 2
    width = time_dev + extra
    freqs = width // 2 + 1
    wide = time_dev + SPAN
    batches, count, parts = channels.shape
    total = batches * count
    rows = total * parts
    forward = np.zeros((wide, 2 * freqs), np.float32)
    forward[:width] = tables(width, freqs, width)
    basis = jnp.asarray(forward.astype(ml_dtypes.bfloat16))
    freq = np.arange(freqs)
    weight = np.where((freq == 0) | (freq == freqs - 1), 1.0, 2.0) / width
    inverse = jnp.asarray(
        (tables(time_dev, freqs, width) * np.concatenate([weight, weight])).T.astype(np.float32)
    )
    devices, windows = lax.axis_size("tmpl"), lax.axis_size("tm")
    copies = 3 * devices // 2
    everyone = devices * records.shape[0]
    vmem = pl.BlockSpec(memory_space=pltpu.VMEM)
    out = pl.pallas_call(
        functools.partial(kernel, devices, windows),
        out_shape=jax.ShapeDtypeStruct((total, time_dev), jnp.float32),
        in_specs=[pl.BlockSpec(memory_space=pltpu.SMEM)] + [vmem] * 2 + [pl.BlockSpec(memory_space=pl.ANY)] * 3,
        out_specs=vmem,
        scratch_shapes=[
            pltpu.VMEM((rows, L), templates.dtype),
            pltpu.VMEM(basis.shape, basis.dtype),
            pltpu.VMEM(inverse.shape, inverse.dtype),
            pltpu.SemaphoreType.DMA((3,)),
            pltpu.VMEM((everyone, wide), records.dtype),
            pltpu.SemaphoreType.DMA((copies,)),
            pltpu.SemaphoreType.DMA((copies,)),
            pltpu.VMEM((rows * SLOTS, LANES), jnp.float32),
            pltpu.VMEM((everyone * SLOTS, LANES), jnp.float32),
            pltpu.VMEM((everyone * SLOTS, LANES), jnp.float32),
            pltpu.VMEM((total * SLOTS, LANES), jnp.float32),
            pltpu.VMEM((total * SLOTS, LANES), jnp.float32),
        ],
        compiler_params=pltpu.CompilerParams(
            collective_id=0, has_side_effects=True, vmem_limit_bytes=56 * 2**20
        ),
    )(
        channels.reshape(total, parts),
        records,
        moveouts.reshape(total, parts),
        templates.reshape(rows, L),
        basis,
        inverse,
    )
    return out.reshape(batches, count, time_dev)


def solution(mesh):
    placed = (
        P("tmpl", "tm"),
        P(None, "tmpl", None, None),
        P(None, "tmpl", None),
        P(None, "tmpl", None),
    )
    return jax.shard_map(
        per_device, mesh=mesh, in_specs=placed, out_specs=P(None, "tmpl", "tm"), check_vma=False
    )
```
